32 devices in a mesh: gx: 8 (over z, y), gy: 4 (over x, core).
Axes of the slice: x: 2, y: 2, z: 4, core: 2. Of those that a mesh axis runs over, the one named last changes fastest.
Arguments:
- embeds: bfloat16 [32, 2048, 768], P('gx', 'gy'), may hold values from -6 to 6
- fetch_list: int32 [2, 8, 8], replicated, may hold values from 0 to 2047, as said below
- partners: int32 [2, 8, 8, 2], replicated, may hold values from 0 to 31, as said below
- counts: int32 [32], replicated, may hold values from 512 to 2048
Outputs:
- nearest: float32 [32, 2048], P('gx', 'gy')
The draws below stay inside these ranges and needn't reach their ends.
Inputs may be any that keep to these rules, and one draw needn't show every extreme that they name: fetch_list[w, h, g] // 64 is a block stored by index g of gx, that is g * 4 <= fetch_list[w, h, g] // 64 < (g + 1) * 4. partners[w, h, g, :] are 2 different blocks stored by index h of gx, none equal to fetch_list[w, h, g] // 64.
All inputs are finite; a program needn't handle non-finite values.
Results may differ from the reference program's by a relative error of at most 0.0003.
Values may be sent and summed in bfloat16 or wider, within the bound.
A program may use at most 192 MiB of HBM per device.

```python
import jax
import jax.numpy as jnp
from jax import lax

D = 768
BLOCK = 2048
OWNED = 4
SLICE = 8
PARTNERS = 2
WAVES = 2
BLOCKS = 32
QUARTER = 512
PIECES = 64
N_GY = 4


def lender_local(key):
    groups = BLOCKS // OWNED
    return jax.random.randint(jax.random.fold_in(key, 11), (WAVES, groups, groups), 0, OWNED)


def draw_fetch_list(key, part):
    groups = BLOCKS // OWNED
    local = lender_local(key)
    piece = jax.random.randint(jax.random.fold_in(key, 37), (WAVES, groups, groups), 0, PIECES)
    owner = jnp.arange(groups, dtype=jnp.int32)[None, None, :] * OWNED
    return ((local + owner) * PIECES + piece).astype(jnp.int32)


def draw_partners(key, part):
    groups = BLOCKS // OWNED
    local = lender_local(key)
    raw = jax.random.randint(jax.random.fold_in(key, 23), (WAVES, groups, groups, OWNED - 1), 0, 1 << 20)
    scores = raw * (OWNED - 1) + jnp.arange(OWNED - 1, dtype=jnp.int32)
    offsets = jnp.argsort(scores, axis=-1)[..., :PARTNERS].astype(jnp.int32) + 1
    chosen = (local[..., None] + offsets) % OWNED
    worker = jnp.arange(groups, dtype=jnp.int32)[None, :, None, None] * OWNED
    return (chosen + worker).astype(jnp.int32)


def place_ends(result, stream_key, least, high):
    spot = [jax.random.randint(jax.random.fold_in(stream_key, axis), (), 0, length) for axis, length in enumerate(result.shape)]
    longest = result.shape.index(max(result.shape))
    next_to = spot[:longest] + [(spot[longest] + 1) % result.shape[longest]] + spot[longest + 1:]
    return result.at[tuple(spot)].set(least).at[tuple(next_to)].set(high)


def shard_levels(key, dims, pieces, smallest, top_value):
    def one(position, blocks):
        heights = jax.random.uniform(jax.random.fold_in(jax.random.fold_in(key, 6), position), (blocks,), jnp.float32, smallest / len(pieces), top_value / len(pieces))
        return jnp.repeat(jnp.exp(heights), dims[position] // blocks).reshape((-1,) + (1,) * (len(dims) - position - 1))

    factor_of = one(*pieces[0])
    for cut in pieces[1:]:
        factor_of = factor_of * one(*cut)
    return factor_of


def noise(own_key, shape, width, limit, split=(), kind=jnp.bfloat16):
    level = shard_levels(own_key, shape, split, -0.22, 0.18) if split else 1.0
    result = jax.random.normal(own_key, shape, jnp.float32) * width * level
    return jnp.minimum(jnp.maximum(result, -limit), limit).astype(kind)


def setup_inputs(seed: int = 0) -> dict:
    arg_keys = jax.random.split(jax.random.key(seed), 5)
    return {
        "embeds": noise(arg_keys[0], (BLOCKS, BLOCK, D), 1.0, 6.0, ((0, 8), (1, 4))),
        "fetch_list": draw_fetch_list(jax.random.fold_in(arg_keys[4], 71), 0),
        "partners": draw_partners(jax.random.fold_in(arg_keys[4], 71), 0),
        "counts": place_ends(jax.random.randint(arg_keys[3], (BLOCKS,), BLOCK // 4, BLOCK + 1), jax.random.fold_in(arg_keys[3], 1), BLOCK // 4, BLOCK).astype(jnp.int32),
    }


EPS = 1e-06

def reference(embeds, fetch_list, partners, counts):
    values = embeds.astype(jnp.float32)
    unit = (values * lax.rsqrt(lax.optimization_barrier(jnp.sum(values * values, axis=-1, keepdims=True)) + EPS)).astype(jnp.bfloat16)
    positions = jnp.arange(embeds.shape[1], dtype=jnp.int32)
    valid = positions[None, :] < counts[:, None]
    lenders = fetch_list.reshape(-1, fetch_list.shape[-1])
    listed = partners.reshape(-1, partners.shape[2], partners.shape[3])
    lanes = jnp.arange(N_GY, dtype=jnp.int32)[:, None] * QUARTER + jnp.arange(SLICE, dtype=jnp.int32)[None, :]
    lanes = lanes.reshape(-1)

    def advance(best, entries):
        tiles, partner_ids = entries
        lent_ids = (tiles // PIECES).astype(jnp.int32)
        piece_ids = (tiles % PIECES).astype(jnp.int32)
        rows = (piece_ids[:, None] * SLICE + lanes[None, :]).astype(jnp.int32)
        owners = jnp.broadcast_to(lent_ids[:, None], rows.shape)
        left = unit[owners, rows].astype(jnp.float32)
        right = unit[partner_ids].astype(jnp.float32)
        scores = jnp.einsum('gqd,gkbd->gqkb', left, right)
        row_ok = rows < counts[lent_ids][:, None]
        keep = row_ok[:, :, None, None] & valid[partner_ids][:, None, :, :]
        scores = jnp.where(keep, scores, jnp.float32(-1.0))
        best = best.at[owners, rows].max(lax.optimization_barrier(jnp.max(scores, axis=(2, 3))))
        best = best.at[partner_ids].max(lax.optimization_barrier(jnp.max(scores, axis=1)))
        return (best, None)
    start = jnp.full(valid.shape, -1.0, jnp.float32)
    best, _ = lax.scan(advance, start, (lenders, listed))
    return jnp.where(valid, best, jnp.float32(-1.0))
```

```python
import functools

import jax
import jax.numpy as jnp
from jax import lax
from jax.experimental import pallas as pl
from jax.experimental.pallas import tpu as pltpu
from jax.sharding import PartitionSpec as P

SLICE = 8
LANES = 128
STEP = 256
EPS = 1e-06
MESH = pl.DeviceIdType.MESH


def unit_rows(values):
    return values * lax.rsqrt(jnp.sum(values * values, axis=-1, keepdims=True) + EPS)


def kernel(
    shape,
    emb_hbm, fetch_hbm, part_hbm, cnt_hbm, out_ref,
    emb, unit, stage, tiles, colacc, rpart, rin, rsum, qin, vecs, fetch, part, cnt,
    load_sem, list_sem,
    send1, recv1, sendx, recvx, sendc, recvc, sendd, recvd, sendr, recvr, sendq, recvq,
):
    groups, owned, quarter, waves = shape
    pieces = quarter // SLICE
    per = waves * SLICE
    own_rows = owned * quarter
    in_tile = LANES // per
    chunks = groups // in_tile
    cs = groups // 8
    me = lax.axis_index("gx")
    lane = lax.axis_index("gy")
    core = lane + 1 - 2 * lax.rem(lane, 2)
    far = lax.rem(lane + 2, 4)
    diag = 3 - lane
    first = me * owned

    loads = []
    for b in range(owned):
        rows = pl.ds(b * quarter // 16, quarter // 16)
        loads.append(pltpu.make_async_copy(emb_hbm.at[rows], emb.at[rows], load_sem.at[b]))
    lists = [
        pltpu.make_async_copy(fetch_hbm, fetch, list_sem.at[0]),
        pltpu.make_async_copy(part_hbm, part, list_sem.at[1]),
        pltpu.make_async_copy(cnt_hbm, cnt, list_sem.at[2]),
    ]
    for copy in lists + loads:
        copy.start()

    barrier = pltpu.get_barrier_semaphore()
    for k in range(1, groups):
        pl.semaphore_signal(
            barrier, inc=1, device_id=(lax.rem(me + k, groups), lane), device_id_type=MESH
        )
    for other in (core, far, diag):
        pl.semaphore_signal(barrier, inc=1, device_id=(me, other), device_id_type=MESH)

    for copy in lists + loads:
        copy.wait()

    def lent(h):
        halves = []
        for w in range(waves):
            local = fetch[w, h, me] - first * pieces
            local = jnp.clip(local, 0, owned * pieces - 1)
            pair = lax.div(local, 2)
            both = emb[pair].astype(jnp.float32)
            odd = jnp.full((SLICE, emb.shape[2]), local - 2 * pair, jnp.int32) == 1
            halves.append(jnp.where(odd, both[SLICE:], both[:SLICE]))
        return unit_rows(jnp.concatenate(halves, axis=0)).astype(jnp.bfloat16)

    def span(g, count=1):
        return pl.ds(pl.multiple_of(g * per, per), count * per)

    def out1(h):
        return pltpu.make_async_remote_copy(
            src_ref=stage.at[span(h)],
            dst_ref=tiles.at[lane, span(me)],
            send_sem=send1.at[h],
            recv_sem=recv1.at[me],
            device_id=(h, lane),
            device_id_type=MESH,
        )

    def in1(g):
        return pltpu.make_async_remote_copy(
            src_ref=stage.at[span(g)],
            dst_ref=tiles.at[lane, span(g)],
            send_sem=send1.at[g],
            recv_sem=recv1.at[g],
            device_id=(g, lane),
            device_id_type=MESH,
        )

    def hop(source, target, c, send, recv):
        part_of = tiles.at[source, span(c * cs, cs)]
        return pltpu.make_async_remote_copy(
            src_ref=part_of,
            dst_ref=part_of,
            send_sem=send.at[c],
            recv_sem=recv.at[c],
            device_id=(me, target),
            device_id_type=MESH,
        )

    for k in range(1, groups):
        h = lax.rem(me + k, groups)
        stage[span(h), :] = lent(h)
        if k == 1:
            pl.semaphore_wait(barrier, groups + 2)
        out1(h).start()
    tiles[lane, span(me), :] = lent(me)

    col = lax.broadcasted_iota(jnp.int32, (8, LANES), 1)
    slot = col // SLICE
    for c in range(chunks):
        limit = jnp.zeros((8, LANES), jnp.int32)
        left = jnp.zeros((8, LANES), jnp.int32)
        right = jnp.zeros((8, LANES), jnp.int32)
        for i in range(in_tile):
            g = c * in_tile + i
            for w in range(waves):
                t = fetch[w, me, g]
                here = slot == i * waves + w
                bound = cnt[lax.div(t, pieces)] - lax.rem(t, pieces) * SLICE
                limit = jnp.where(here, bound, limit)
                left = jnp.where(here, part[w, me, 0, g] - first, left)
                right = jnp.where(here, part[w, me, 1, g] - first, right)
        vecs[c, 0] = limit - lax.rem(col, SLICE)
        vecs[c, 1] = left
        vecs[c, 2] = right

    rows_each = 64

    def own(i, carry):
        at = pl.ds(pl.multiple_of(i * rows_each, rows_each), rows_each)
        held = emb[pl.ds(i * (rows_each // 16), rows_each // 16)].astype(jnp.float32)
        unit[at, :] = unit_rows(held.reshape(rows_each, -1)).astype(jnp.bfloat16)
        return carry

    lax.fori_loop(0, own_rows // rows_each, own, 0)

    home = lax.div(me, cs)
    order = [lax.rem(home + 8 - k, 8) for k in range(8)]
    for k, c in enumerate(order):
        for i in range(cs):
            g = c * cs + i
            if cs == 1:
                if k:
                    in1(g).wait_recv()
            else:
                pl.when(g != me)(lambda g=g: in1(g).wait_recv())
        hop(lane, far, c, sendx, recvx).start()
        hop(lane, core, c, sendc, recvc).start()

    def score(la, lb, begin):
        def one(c, carry):
            rows = pl.ds(pl.multiple_of(c * LANES, LANES), LANES)
            tile = jnp.concatenate([tiles[la, rows, :], tiles[lb, rows, :]], axis=0)
            limit, left, right = vecs[c, 0], vecs[c, 1], vecs[c, 2]
            within = jnp.concatenate([limit - la * quarter, limit - lb * quarter], axis=1)
            pick_l = jnp.concatenate([left, left], axis=1)
            pick_r = jnp.concatenate([right, right], axis=1)
            best = jnp.full((8, 2 * LANES), -1.0, jnp.float32)
            for j in range(own_rows // STEP):
                b, offset = divmod(j * STEP, quarter)
                at = pl.ds(j * STEP, STEP)
                s = lax.dot_general(
                    unit[at, :], tile, (((1,), (1,)), ((), ())), preferred_element_type=jnp.float32
                )
                picked = (within > 0) & ((pick_l == b) | (pick_r == b))
                place = lax.broadcasted_iota(jnp.int32, (STEP, 2 * LANES), 0)
                seen = place < cnt[first + b] - lane * quarter - offset
                masked = jnp.where(seen, s, -1.0).reshape(STEP // 8, 8, 2 * LANES)
                best = jnp.maximum(best, jnp.where(picked, jnp.max(masked, axis=0), -1.0))
                s = jnp.where(picked[None], s.reshape(STEP // 8, 8, 2 * LANES), -1.0)
                s = s.reshape(STEP, 2 * LANES)
                s = jnp.maximum(s[:, :LANES], s[:, LANES:])
                if begin and chunks == 1:
                    colacc[at, :] = s
                else:
                    colacc[at, :] = jnp.maximum(colacc[at, :], s)
            rpart[la, c] = best[:, :LANES]
            rpart[lb, c] = best[:, LANES:]
            return carry

        if chunks == 1:
            one(0, 0)
        else:
            lax.fori_loop(0, chunks, one, 0)

    if chunks > 1:
        colacc[...] = jnp.full(colacc.shape, -1.0, jnp.float32)

    def give(target, i):
        return pltpu.make_async_remote_copy(
            src_ref=rpart.at[target],
            dst_ref=rin.at[lane],
            send_sem=sendr.at[i],
            recv_sem=recvr.at[i],
            device_id=(me, target),
            device_id_type=MESH,
        )

    def take(source, i):
        return pltpu.make_async_remote_copy(
            src_ref=rpart.at[source],
            dst_ref=rin.at[source],
            send_sem=sendr.at[i],
            recv_sem=recvr.at[i],
            device_id=(me, source),
            device_id_type=MESH,
        )

    for c in order:
        hop(core, core, c, sendc, recvc).wait_recv()
    score(lane, core, True)
    give(core, 0).start()
    for c in order:
        hop(far, far, c, sendx, recvx).wait_recv()
        hop(far, core, c, sendd, recvd).start()
    for c in order:
        hop(diag, core, c, sendd, recvd).wait_recv()
    score(far, diag, False)
    give(far, 1).start()
    give(diag, 2).start()

    best = rpart[lane]
    for i, other in enumerate((core, far, diag)):
        take(other, i).wait_recv()
        best = jnp.maximum(best, rin[other])
    rsum[...] = best

    def back(g):
        return pltpu.make_async_remote_copy(
            src_ref=rsum.at[lax.div(g, in_tile)],
            dst_ref=qin.at[me],
            send_sem=sendq.at[g],
            recv_sem=recvq.at[me],
            device_id=(g, lane),
            device_id_type=MESH,
        )

    def home_again(h):
        return pltpu.make_async_remote_copy(
            src_ref=rsum.at[lax.div(h, in_tile)],
            dst_ref=qin.at[h],
            send_sem=sendq.at[h],
            recv_sem=recvq.at[h],
            device_id=(h, lane),
            device_id_type=MESH,
        )

    for k in range(1, groups):
        back(lax.rem(me + k, groups)).start()
    qin[me] = rsum[lax.div(me, in_tile)]

    lines = own_rows // LANES
    total = jnp.concatenate(
        [
            jnp.max(colacc[i * LANES:(i + 1) * LANES, :].T, axis=0, keepdims=True)
            for i in range(lines)
        ],
        axis=0,
    )

    for k in range(1, groups):
        home_again(lax.rem(me + groups - k, groups)).wait_recv()

    spot = lax.broadcasted_iota(jnp.int32, (lines, LANES), 0) * (LANES // SLICE)
    spot = spot + lax.broadcasted_iota(jnp.int32, (lines, LANES), 1) // SLICE
    mine = lax.rem(me, in_tile) * waves
    for h0 in range(0, groups, 8):
        rows8 = jnp.max(qin[h0:h0 + 8], axis=1)
        for w in range(waves):
            x = jnp.where(slot == mine + w, rows8, -1.0)
            for shift in (8, 16, 32, 64):
                x = jnp.maximum(x, pltpu.roll(x, shift, 1))
            for i in range(8):
                local = fetch[w, h0 + i, me] - first * pieces
                total = jnp.maximum(total, jnp.where(spot == local, x[i:i + 1], -1.0))

    each = quarter // LANES
    for i in range(lines):
        b, q = divmod(i, each)
        place = lax.broadcasted_iota(jnp.int32, (1, LANES), 1) + (lane * quarter + q * LANES)
        line = jnp.where(place < cnt[first + b], jnp.maximum(total[i:i + 1], -1.0), -1.0)
        out_ref[b:b + 1, q * LANES:(q + 1) * LANES] = line

    for k in range(1, groups):
        h = lax.rem(me + k, groups)
        out1(h).wait_send()
        back(h).wait_send()
    for c in order:
        hop(lane, far, c, sendx, recvx).wait_send()
        hop(lane, core, c, sendc, recvc).wait_send()
        hop(far, core, c, sendd, recvd).wait_send()
    for i, other in enumerate((core, far, diag)):
        give(other, i).wait_send()


def on_device(embeds, fetch_list, partners, counts):
    owned, quarter, width = embeds.shape
    waves, groups, _ = fetch_list.shape
    own_rows = owned * quarter
    per = waves * SLICE
    chunks = groups * per // LANES
    listed = jnp.transpose(partners, (0, 1, 3, 2))
    anywhere = pl.BlockSpec(memory_space=pl.ANY)
    dma = pltpu.SemaphoreType.DMA
    flops = 2 * 4 * groups * per * own_rows * width
    return pl.pallas_call(
        functools.partial(kernel, (groups, owned, quarter, waves)),
        out_shape=jax.ShapeDtypeStruct((owned, quarter), jnp.float32),
        in_specs=[anywhere] * 4,
        out_specs=pl.BlockSpec(memory_space=pltpu.VMEM),
        scratch_shapes=[
            pltpu.VMEM((own_rows // 16, 16, width), jnp.bfloat16),
            pltpu.VMEM((own_rows, width), jnp.bfloat16),
            pltpu.VMEM((groups * per, width), jnp.bfloat16),
            pltpu.VMEM((4, groups * per, width), jnp.bfloat16),
            pltpu.VMEM((own_rows, LANES), jnp.float32),
            pltpu.VMEM((4, chunks, 8, LANES), jnp.float32),
            pltpu.VMEM((4, chunks, 8, LANES), jnp.float32),
            pltpu.VMEM((chunks, 8, LANES), jnp.float32),
            pltpu.VMEM((groups, 8, LANES), jnp.float32),
            pltpu.VMEM((chunks, 3, 8, LANES), jnp.int32),
            pltpu.SMEM(fetch_list.shape, jnp.int32),
            pltpu.SMEM(listed.shape, jnp.int32),
            pltpu.SMEM(counts.shape, jnp.int32),
            dma((owned,)),
            dma((3,)),
            dma((groups,)),
            dma((groups,)),
            dma((8,)),
            dma((8,)),
            dma((8,)),
            dma((8,)),
            dma((8,)),
            dma((8,)),
            dma((3,)),
            dma((3,)),
            dma((groups,)),
            dma((groups,)),
        ],
        compiler_params=pltpu.CompilerParams(
            collective_id=0, has_side_effects=True, vmem_limit_bytes=60 * 2**20
        ),
        cost_estimate=pl.CostEstimate(
            flops=flops, bytes_accessed=own_rows * width * 2, transcendentals=0
        ),
    )(embeds.reshape(own_rows // 16, 16, width), fetch_list, listed, counts)


def solution(mesh):
    in_specs = (P("gx", "gy", None), P(), P(), P())
    out_specs = P("gx", "gy")
    return jax.shard_map(
        on_device, mesh=mesh, in_specs=in_specs, out_specs=out_specs, check_vma=False
    )
```

```python
import functools

import jax
import jax.numpy as jnp
from jax import lax
from jax.experimental import pallas as pl
from jax.experimental.pallas import tpu as pltpu
from jax.sharding import PartitionSpec as P

SLICE = 8
LANES = 128
STEP = 256
EPS = 1e-06
MESH = pl.DeviceIdType.MESH


def unit_rows(values):
    return values * lax.rsqrt(jnp.sum(values * values, axis=-1, keepdims=True) + EPS)


def kernel(
    shape,
    emb_hbm, fetch_hbm, part_hbm, cnt_hbm, out_ref,
    emb, unit, stage, tiles, colacc, rpart, qin, vecs, fetch, part, cnt,
    load_sem, list_sem,
    send1, recv1, sendx, recvx, sendc, recvc, sendd, recvd, sendr, recvr, sendn, recvn,
):
    groups, owned, quarter, waves = shape
    pieces = quarter // SLICE
    per = waves * SLICE
    own_rows = owned * quarter
    in_tile = LANES // per
    chunks = groups // in_tile
    cs = groups // 8
    me = lax.axis_index("gx")
    lane = lax.axis_index("gy")
    core = lane + 1 - 2 * lax.rem(lane, 2)
    far = lax.rem(lane + 2, 4)
    diag = 3 - lane
    first = me * owned

    loads = []
    for b in range(owned):
        rows = pl.ds(b * quarter // 16, quarter // 16)
        loads.append(pltpu.make_async_copy(emb_hbm.at[rows], emb.at[rows], load_sem.at[b]))
    lists = [
        pltpu.make_async_copy(fetch_hbm, fetch, list_sem.at[0]),
        pltpu.make_async_copy(part_hbm, part, list_sem.at[1]),
        pltpu.make_async_copy(cnt_hbm, cnt, list_sem.at[2]),
    ]
    for copy in lists + loads:
        copy.start()

    barrier = pltpu.get_barrier_semaphore()
    for k in range(groups):
        for other in (lane, core, far, diag):
            if k or other is not lane:
                pl.semaphore_signal(
                    barrier, inc=1, device_id=(lax.rem(me + k, groups), other), device_id_type=MESH
                )

    for copy in lists + loads:
        copy.wait()

    def lent(h):
        halves = []
        for w in range(waves):
            local = fetch[w, h, me] - first * pieces
            local = jnp.clip(local, 0, owned * pieces - 1)
            pair = lax.div(local, 2)
            both = emb[pair].astype(jnp.float32)
            odd = jnp.full((SLICE, emb.shape[2]), local - 2 * pair, jnp.int32) == 1
            halves.append(jnp.where(odd, both[SLICE:], both[:SLICE]))
        return unit_rows(jnp.concatenate(halves, axis=0)).astype(jnp.bfloat16)

    def span(g, count=1):
        return pl.ds(pl.multiple_of(g * per, per), count * per)

    def out1(h):
        return pltpu.make_async_remote_copy(
            src_ref=stage.at[span(h)],
            dst_ref=tiles.at[lane, span(me)],
            send_sem=send1.at[h],
            recv_sem=recv1.at[me],
            device_id=(h, lane),
            device_id_type=MESH,
        )

    def in1(g):
        return pltpu.make_async_remote_copy(
            src_ref=stage.at[span(g)],
            dst_ref=tiles.at[lane, span(g)],
            send_sem=send1.at[g],
            recv_sem=recv1.at[g],
            device_id=(g, lane),
            device_id_type=MESH,
        )

    def hop(source, target, c, send, recv):
        part_of = tiles.at[source, span(c * cs, cs)]
        return pltpu.make_async_remote_copy(
            src_ref=part_of,
            dst_ref=part_of,
            send_sem=send.at[c],
            recv_sem=recv.at[c],
            device_id=(me, target),
            device_id_type=MESH,
        )

    for k in range(1, groups):
        h = lax.rem(me + k, groups)
        stage[span(h), :] = lent(h)
        if k == 1:
            pl.semaphore_wait(barrier, 4 * groups - 1)
        out1(h).start()
    tiles[lane, span(me), :] = lent(me)

    col = lax.broadcasted_iota(jnp.int32, (8, LANES), 1)
    slot = col // SLICE
    for c in range(chunks):
        limit = jnp.zeros((8, LANES), jnp.int32)
        left = jnp.zeros((8, LANES), jnp.int32)
        right = jnp.zeros((8, LANES), jnp.int32)
        for i in range(in_tile):
            g = c * in_tile + i
            for w in range(waves):
                t = fetch[w, me, g]
                here = slot == i * waves + w
                bound = cnt[lax.div(t, pieces)] - lax.rem(t, pieces) * SLICE
                limit = jnp.where(here, bound, limit)
                left = jnp.where(here, part[w, me, 0, g] - first, left)
                right = jnp.where(here, part[w, me, 1, g] - first, right)
        vecs[c, 0] = limit - lax.rem(col, SLICE)
        vecs[c, 1] = left
        vecs[c, 2] = right

    rows_each = 64

    def own(i, carry):
        at = pl.ds(pl.multiple_of(i * rows_each, rows_each), rows_each)
        held = emb[pl.ds(i * (rows_each // 16), rows_each // 16)].astype(jnp.float32)
        unit[at, :] = unit_rows(held.reshape(rows_each, -1)).astype(jnp.bfloat16)
        return carry

    lax.fori_loop(0, own_rows // rows_each, own, 0)

    home = lax.div(me, cs)
    order = [lax.rem(home + 8 - k, 8) for k in range(8)]
    for k, c in enumerate(order):
        for i in range(cs):
            g = c * cs + i
            if cs == 1:
                if k:
                    in1(g).wait_recv()
            else:
                pl.when(g != me)(lambda g=g: in1(g).wait_recv())
        hop(lane, far, c, sendx, recvx).start()
        hop(lane, core, c, sendc, recvc).start()

    def score(la, lb, begin):
        def one(c, carry):
            rows = pl.ds(pl.multiple_of(c * LANES, LANES), LANES)
            tile = jnp.concatenate([tiles[la, rows, :], tiles[lb, rows, :]], axis=0)
            limit, left, right = vecs[c, 0], vecs[c, 1], vecs[c, 2]
            within = jnp.concatenate([limit - la * quarter, limit - lb * quarter], axis=1)
            pick_l = jnp.concatenate([left, left], axis=1)
            pick_r = jnp.concatenate([right, right], axis=1)
            best = jnp.full((8, 2 * LANES), -1.0, jnp.float32)
            for j in range(own_rows // STEP):
                b, offset = divmod(j * STEP, quarter)
                at = pl.ds(j * STEP, STEP)
                s = lax.dot_general(
                    unit[at, :], tile, (((1,), (1,)), ((), ())), preferred_element_type=jnp.float32
                )
                picked = (within > 0) & ((pick_l == b) | (pick_r == b))
                place = lax.broadcasted_iota(jnp.int32, (STEP, 2 * LANES), 0)
                seen = place < cnt[first + b] - lane * quarter - offset
                masked = jnp.where(seen, s, -1.0).reshape(STEP // 8, 8, 2 * LANES)
                best = jnp.maximum(best, jnp.where(picked, jnp.max(masked, axis=0), -1.0))
                s = jnp.where(picked[None], s.reshape(STEP // 8, 8, 2 * LANES), -1.0)
                s = s.reshape(STEP, 2 * LANES)
                s = jnp.maximum(s[:, :LANES], s[:, LANES:])
                if begin and chunks == 1:
                    colacc[at, :] = s
                else:
                    colacc[at, :] = jnp.maximum(colacc[at, :], s)
            best = jnp.broadcast_to(jnp.max(best, axis=0, keepdims=True), best.shape)
            rpart[la, c] = best[:, :LANES]
            rpart[lb, c] = best[:, LANES:]
            return carry

        if chunks == 1:
            one(0, 0)
        else:
            lax.fori_loop(0, chunks, one, 0)

    if chunks > 1:
        colacc[...] = jnp.full(colacc.shape, -1.0, jnp.float32)

    def answer(g, target):
        at = lax.div(me, 8), pl.ds(lax.rem(me, 8), 1)
        send = sendn.at[g] if target is lane else sendr.at[target]
        recv = recvn.at[me] if target is lane else recvr.at[lane]
        return pltpu.make_async_remote_copy(
            src_ref=rpart.at[target, lax.div(g, in_tile), pl.ds(0, 1)],
            dst_ref=qin.at[(lane, *at)],
            send_sem=send,
            recv_sem=recv,
            device_id=(g, target),
            device_id_type=MESH,
        )

    def answered(h):
        return pltpu.make_async_remote_copy(
            src_ref=rpart.at[lane, lax.div(h, in_tile), pl.ds(0, 1)],
            dst_ref=qin.at[lane, lax.div(h, 8), pl.ds(lax.rem(h, 8), 1)],
            send_sem=sendn.at[h],
            recv_sem=recvn.at[h],
            device_id=(h, lane),
            device_id_type=MESH,
        )

    def all_of(other):
        return pltpu.make_async_remote_copy(
            src_ref=rpart.at[other],
            dst_ref=qin.at[other],
            send_sem=sendr.at[other],
            recv_sem=recvr.at[other],
            device_id=(me, other),
            device_id_type=MESH,
        )

    def reply(target):
        for k in range(1, groups):
            answer(lax.rem(me + k, groups), target).start()
        if target is not lane:
            answer(me, target).start()

    for c in order:
        hop(core, core, c, sendc, recvc).wait_recv()
    score(lane, core, True)
    reply(core)
    reply(lane)
    mine_row = rpart[lane, lax.div(me, in_tile), pl.ds(0, 1)]
    qin[lane, lax.div(me, 8), pl.ds(lax.rem(me, 8), 1)] = mine_row
    for c in order:
        hop(far, far, c, sendx, recvx).wait_recv()
        hop(far, core, c, sendd, recvd).start()
    for c in order:
        hop(diag, core, c, sendd, recvd).wait_recv()
    score(far, diag, False)
    reply(far)
    reply(diag)

    lines = own_rows // LANES
    total = jnp.concatenate(
        [
            jnp.max(colacc[i * LANES:(i + 1) * LANES, :].T, axis=0, keepdims=True)
            for i in range(lines)
        ],
        axis=0,
    )

    for k in range(1, groups):
        answered(lax.rem(me + groups - k, groups)).wait_recv()
    for other in (core, far, diag):
        all_of(other).wait_recv()

    spot = lax.broadcasted_iota(jnp.int32, (lines, LANES), 0) * (LANES // SLICE)
    spot = spot + lax.broadcasted_iota(jnp.int32, (lines, LANES), 1) // SLICE
    mine = lax.rem(me, in_tile) * waves
    for h0 in range(0, groups, 8):
        rows8 = jnp.maximum(qin[0, h0 // 8], qin[1, h0 // 8])
        rows8 = jnp.maximum(rows8, jnp.maximum(qin[2, h0 // 8], qin[3, h0 // 8]))
        for w in range(waves):
            x = jnp.where(slot == mine + w, rows8, -1.0)
            for shift in (8, 16, 32, 64):
                x = jnp.maximum(x, pltpu.roll(x, shift, 1))
            for i in range(8):
                local = fetch[w, h0 + i, me] - first * pieces
                total = jnp.maximum(total, jnp.where(spot == local, x[i:i + 1], -1.0))

    each = quarter // LANES
    for i in range(lines):
        b, q = divmod(i, each)
        place = lax.broadcasted_iota(jnp.int32, (1, LANES), 1) + (lane * quarter + q * LANES)
        line = jnp.where(place < cnt[first + b], jnp.maximum(total[i:i + 1], -1.0), -1.0)
        out_ref[b:b + 1, q * LANES:(q + 1) * LANES] = line

    for k in range(1, groups):
        h = lax.rem(me + k, groups)
        out1(h).wait_send()
        answered(h).wait_send()
    for c in order:
        hop(lane, far, c, sendx, recvx).wait_send()
        hop(lane, core, c, sendc, recvc).wait_send()
        hop(far, core, c, sendd, recvd).wait_send()
    for other in (core, far, diag):
        all_of(other).wait_send()


def on_device(embeds, fetch_list, partners, counts):
    owned, quarter, width = embeds.shape
    waves, groups, _ = fetch_list.shape
    own_rows = owned * quarter
    per = waves * SLICE
    chunks = groups * per // LANES
    listed = jnp.transpose(partners, (0, 1, 3, 2))
    anywhere = pl.BlockSpec(memory_space=pl.ANY)
    dma = pltpu.SemaphoreType.DMA
    flops = 2 * 4 * groups * per * own_rows * width
    return pl.pallas_call(
        functools.partial(kernel, (groups, owned, quarter, waves)),
        out_shape=jax.ShapeDtypeStruct((owned, quarter), jnp.float32),
        in_specs=[anywhere] * 4,
        out_specs=pl.BlockSpec(memory_space=pltpu.VMEM),
        scratch_shapes=[
            pltpu.VMEM((own_rows // 16, 16, width), jnp.bfloat16),
            pltpu.VMEM((own_rows, width), jnp.bfloat16),
            pltpu.VMEM((groups * per, width), jnp.bfloat16),
            pltpu.VMEM((4, groups * per, width), jnp.bfloat16),
            pltpu.VMEM((own_rows, LANES), jnp.float32),
            pltpu.VMEM((4, chunks, 8, LANES), jnp.float32),
            pltpu.VMEM((4, groups // 8, 8, LANES), jnp.float32),
            pltpu.VMEM((chunks, 3, 8, LANES), jnp.int32),
            pltpu.SMEM(fetch_list.shape, jnp.int32),
            pltpu.SMEM(listed.shape, jnp.int32),
            pltpu.SMEM(counts.shape, jnp.int32),
            dma((owned,)),
            dma((3,)),
            dma((groups,)),
            dma((groups,)),
            dma((8,)),
            dma((8,)),
            dma((8,)),
            dma((8,)),
            dma((8,)),
            dma((8,)),
            dma((4,)),
            dma((4,)),
            dma((groups,)),
            dma((groups,)),
        ],
        compiler_params=pltpu.CompilerParams(
            collective_id=0, has_side_effects=True, vmem_limit_bytes=60 * 2**20
        ),
        cost_estimate=pl.CostEstimate(
            flops=flops, bytes_accessed=own_rows * width * 2, transcendentals=0
        ),
    )(embeds.reshape(own_rows // 16, 16, width), fetch_list, listed, counts)


def solution(mesh):
    in_specs = (P("gx", "gy", None), P(), P(), P())
    out_specs = P("gx", "gy")
    return jax.shard_map(
        on_device, mesh=mesh, in_specs=in_specs, out_specs=out_specs, check_vma=False
    )
```

```python
import functools

import jax
import jax.numpy as jnp
from jax import lax
from jax.experimental import pallas as pl
from jax.experimental.pallas import tpu as pltpu
from jax.sharding import PartitionSpec as P

SLICE = 8
LANES = 128
STEP = 256
EPS = 1e-06
MESH = pl.DeviceIdType.MESH


def unit_rows(values):
    return values * lax.rsqrt(jnp.sum(values * values, axis=-1, keepdims=True) + EPS)


def outward(n):
    return sorted(range(1, n), key=lambda k: (abs(2 * k - n), k))


def kernel(
    shape,
    emb_hbm, fetch_hbm, part_hbm, cnt_hbm, out_ref,
    emb, unit, stage, tiles, colacc, rpart, qin, vecs, fetch, part, cnt,
    load_sem, list_sem,
    send1, recv1, sendx, recvx, sendc, recvc, sendd, recvd, sendr, recvr, sendn, recvn,
):
    groups, owned, quarter, waves = shape
    pieces = quarter // SLICE
    per = waves * SLICE
    own_rows = owned * quarter
    in_tile = LANES // per
    chunks = groups // in_tile
    cs = groups // 8
    me = lax.axis_index("gx")
    lane = lax.axis_index("gy")
    core = lane + 1 - 2 * lax.rem(lane, 2)
    far = lax.rem(lane + 2, 4)
    diag = 3 - lane
    first = me * owned
    far_first = outward(groups)

    loads = []
    for b in range(owned):
        rows = pl.ds(b * quarter // 16, quarter // 16)
        loads.append(pltpu.make_async_copy(emb_hbm.at[rows], emb.at[rows], load_sem.at[b]))
    lists = [
        pltpu.make_async_copy(fetch_hbm, fetch, list_sem.at[0]),
        pltpu.make_async_copy(part_hbm, part, list_sem.at[1]),
        pltpu.make_async_copy(cnt_hbm, cnt, list_sem.at[2]),
    ]
    for copy in lists + loads:
        copy.start()

    barrier = pltpu.get_barrier_semaphore()
    for k in range(groups):
        for other in (lane, core, far, diag):
            if (other is lane) != (k == 0):
                pl.semaphore_signal(
                    barrier, inc=1, device_id=(lax.rem(me + k, groups), other), device_id_type=MESH
                )

    for copy in lists + loads:
        copy.wait()

    def lent(h):
        halves = []
        for w in range(waves):
            local = fetch[w, h, me] - first * pieces
            local = jnp.clip(local, 0, owned * pieces - 1)
            pair = lax.div(local, 2)
            both = emb[pair].astype(jnp.float32)
            odd = jnp.full((SLICE, emb.shape[2]), local - 2 * pair, jnp.int32) == 1
            halves.append(jnp.where(odd, both[SLICE:], both[:SLICE]))
        return unit_rows(jnp.concatenate(halves, axis=0)).astype(jnp.bfloat16)

    def span(g, count=1):
        return pl.ds(pl.multiple_of(g * per, per), count * per)

    def out1(h):
        return pltpu.make_async_remote_copy(
            src_ref=stage.at[span(h)],
            dst_ref=tiles.at[lane, span(me)],
            send_sem=send1.at[h],
            recv_sem=recv1.at[me],
            device_id=(h, lane),
            device_id_type=MESH,
        )

    def in1(g):
        return pltpu.make_async_remote_copy(
            src_ref=stage.at[span(g)],
            dst_ref=tiles.at[lane, span(g)],
            send_sem=send1.at[g],
            recv_sem=recv1.at[g],
            device_id=(g, lane),
            device_id_type=MESH,
        )

    def hop(source, target, c, send, recv):
        part_of = tiles.at[source, span(c * cs, cs)]
        return pltpu.make_async_remote_copy(
            src_ref=part_of,
            dst_ref=part_of,
            send_sem=send.at[c],
            recv_sem=recv.at[c],
            device_id=(me, target),
            device_id_type=MESH,
        )

    for n, k in enumerate(far_first):
        h = lax.rem(me + k, groups)
        stage[span(h), :] = lent(h)
        if n == 0:
            pl.semaphore_wait(barrier, groups + 2)
        out1(h).start()
    tiles[lane, span(me), :] = lent(me)

    col = lax.broadcasted_iota(jnp.int32, (8, LANES), 1)
    slot = col // SLICE
    for c in range(chunks):
        limit = jnp.zeros((8, LANES), jnp.int32)
        left = jnp.zeros((8, LANES), jnp.int32)
        right = jnp.zeros((8, LANES), jnp.int32)
        for i in range(in_tile):
            g = c * in_tile + i
            for w in range(waves):
                t = fetch[w, me, g]
                here = slot == i * waves + w
                bound = cnt[lax.div(t, pieces)] - lax.rem(t, pieces) * SLICE
                limit = jnp.where(here, bound, limit)
                left = jnp.where(here, part[w, me, 0, g] - first, left)
                right = jnp.where(here, part[w, me, 1, g] - first, right)
        vecs[c, 0] = limit - lax.rem(col, SLICE)
        vecs[c, 1] = left
        vecs[c, 2] = right

    rows_each = 64

    def own(i, carry):
        at = pl.ds(pl.multiple_of(i * rows_each, rows_each), rows_each)
        held = emb[pl.ds(i * (rows_each // 16), rows_each // 16)].astype(jnp.float32)
        unit[at, :] = unit_rows(held.reshape(rows_each, -1)).astype(jnp.bfloat16)
        return carry

    lax.fori_loop(0, own_rows // rows_each, own, 0)

    home = lax.div(me, cs)
    order = [lax.rem(home + 8 - k, 8) for k in [0, *outward(8)]]
    for k, c in enumerate(order):
        for i in range(cs):
            g = c * cs + i
            if cs == 1:
                if k:
                    in1(g).wait_recv()
            else:
                pl.when(g != me)(lambda g=g: in1(g).wait_recv())
        hop(lane, far, c, sendx, recvx).start()
        hop(lane, core, c, sendc, recvc).start()

    def score(la, lb, begin):
        def one(c, carry):
            rows = pl.ds(pl.multiple_of(c * LANES, LANES), LANES)
            tile = jnp.concatenate([tiles[la, rows, :], tiles[lb, rows, :]], axis=0)
            limit, left, right = vecs[c, 0], vecs[c, 1], vecs[c, 2]
            within = jnp.concatenate([limit - la * quarter, limit - lb * quarter], axis=1)
            pick_l = jnp.concatenate([left, left], axis=1)
            pick_r = jnp.concatenate([right, right], axis=1)
            best = jnp.full((8, 2 * LANES), -1.0, jnp.float32)
            for j in range(own_rows // STEP):
                b, offset = divmod(j * STEP, quarter)
                at = pl.ds(j * STEP, STEP)
                s = lax.dot_general(
                    unit[at, :], tile, (((1,), (1,)), ((), ())), preferred_element_type=jnp.float32
                )
                picked = (within > 0) & ((pick_l == b) | (pick_r == b))
                place = lax.broadcasted_iota(jnp.int32, (STEP, 2 * LANES), 0)
                seen = place < cnt[first + b] - lane * quarter - offset
                masked = jnp.where(seen, s, -1.0).reshape(STEP // 8, 8, 2 * LANES)
                best = jnp.maximum(best, jnp.where(picked, jnp.max(masked, axis=0), -1.0))
                s = jnp.where(picked[None], s.reshape(STEP // 8, 8, 2 * LANES), -1.0)
                s = s.reshape(STEP, 2 * LANES)
                s = jnp.maximum(s[:, :LANES], s[:, LANES:])
                if begin and chunks == 1:
                    colacc[at, :] = s
                else:
                    colacc[at, :] = jnp.maximum(colacc[at, :], s)
            best = jnp.broadcast_to(jnp.max(best, axis=0, keepdims=True), best.shape)
            rpart[la, c] = best[:, :LANES]
            rpart[lb, c] = best[:, LANES:]
            return carry

        if chunks == 1:
            one(0, 0)
        else:
            lax.fori_loop(0, chunks, one, 0)

    if chunks > 1:
        colacc[...] = jnp.full(colacc.shape, -1.0, jnp.float32)

    def answer(g, target):
        at = lax.div(me, 8), pl.ds(lax.rem(me, 8), 1)
        send = sendn.at[g] if target is lane else sendr.at[target]
        recv = recvn.at[me] if target is lane else recvr.at[lane]
        return pltpu.make_async_remote_copy(
            src_ref=rpart.at[target, lax.div(g, in_tile), pl.ds(0, 1)],
            dst_ref=qin.at[(lane, *at)],
            send_sem=send,
            recv_sem=recv,
            device_id=(g, target),
            device_id_type=MESH,
        )

    def answered(h):
        return pltpu.make_async_remote_copy(
            src_ref=rpart.at[lane, lax.div(h, in_tile), pl.ds(0, 1)],
            dst_ref=qin.at[lane, lax.div(h, 8), pl.ds(lax.rem(h, 8), 1)],
            send_sem=sendn.at[h],
            recv_sem=recvn.at[h],
            device_id=(h, lane),
            device_id_type=MESH,
        )

    def all_of(other):
        return pltpu.make_async_remote_copy(
            src_ref=rpart.at[other],
            dst_ref=qin.at[other],
            send_sem=sendr.at[other],
            recv_sem=recvr.at[other],
            device_id=(me, other),
            device_id_type=MESH,
        )

    def reply(target):
        for k in far_first:
            answer(lax.rem(me + k, groups), target).start()
        if target is not lane:
            answer(me, target).start()

    for c in order:
        hop(core, core, c, sendc, recvc).wait_recv()
    score(lane, core, True)
    reply(core)
    reply(lane)
    mine_row = rpart[lane, lax.div(me, in_tile), pl.ds(0, 1)]
    qin[lane, lax.div(me, 8), pl.ds(lax.rem(me, 8), 1)] = mine_row
    for c in order:
        hop(far, far, c, sendx, recvx).wait_recv()
        hop(far, core, c, sendd, recvd).start()
    for c in order:
        hop(diag, core, c, sendd, recvd).wait_recv()
    score(far, diag, False)
    reply(far)
    reply(diag)

    lines = own_rows // LANES
    total = jnp.concatenate(
        [
            jnp.max(colacc[i * LANES:(i + 1) * LANES, :].T, axis=0, keepdims=True)
            for i in range(lines)
        ],
        axis=0,
    )

    for k in range(1, groups):
        answered(lax.rem(me + groups - k, groups)).wait_recv()
    for other in (core, far, diag):
        all_of(other).wait_recv()

    spot = lax.broadcasted_iota(jnp.int32, (lines, LANES), 0) * (LANES // SLICE)
    spot = spot + lax.broadcasted_iota(jnp.int32, (lines, LANES), 1) // SLICE
    mine = lax.rem(me, in_tile) * waves
    for h0 in range(0, groups, 8):
        rows8 = jnp.maximum(qin[0, h0 // 8], qin[1, h0 // 8])
        rows8 = jnp.maximum(rows8, jnp.maximum(qin[2, h0 // 8], qin[3, h0 // 8]))
        for w in range(waves):
            x = jnp.where(slot == mine + w, rows8, -1.0)
            for shift in (8, 16, 32, 64):
                x = jnp.maximum(x, pltpu.roll(x, shift, 1))
            for i in range(8):
                local = fetch[w, h0 + i, me] - first * pieces
                total = jnp.maximum(total, jnp.where(spot == local, x[i:i + 1], -1.0))

    each = quarter // LANES
    for i in range(lines):
        b, q = divmod(i, each)
        place = lax.broadcasted_iota(jnp.int32, (1, LANES), 1) + (lane * quarter + q * LANES)
        line = jnp.where(place < cnt[first + b], jnp.maximum(total[i:i + 1], -1.0), -1.0)
        out_ref[b:b + 1, q * LANES:(q + 1) * LANES] = line

    for k in range(1, groups):
        h = lax.rem(me + k, groups)
        out1(h).wait_send()
        answered(h).wait_send()
    for c in order:
        hop(lane, far, c, sendx, recvx).wait_send()
        hop(lane, core, c, sendc, recvc).wait_send()
        hop(far, core, c, sendd, recvd).wait_send()
    for other in (core, far, diag):
        all_of(other).wait_send()


def on_device(embeds, fetch_list, partners, counts):
    owned, quarter, width = embeds.shape
    waves, groups, _ = fetch_list.shape
    own_rows = owned * quarter
    per = waves * SLICE
    chunks = groups * per // LANES
    listed = jnp.transpose(partners, (0, 1, 3, 2))
    anywhere = pl.BlockSpec(memory_space=pl.ANY)
    dma = pltpu.SemaphoreType.DMA
    flops = 2 * 4 * groups * per * own_rows * width
    return pl.pallas_call(
        functools.partial(kernel, (groups, owned, quarter, waves)),
        out_shape=jax.ShapeDtypeStruct((owned, quarter), jnp.float32),
        in_specs=[anywhere] * 4,
        out_specs=pl.BlockSpec(memory_space=pltpu.VMEM),
        scratch_shapes=[
            pltpu.VMEM((own_rows // 16, 16, width), jnp.bfloat16),
            pltpu.VMEM((own_rows, width), jnp.bfloat16),
            pltpu.VMEM((groups * per, width), jnp.bfloat16),
            pltpu.VMEM((4, groups * per, width), jnp.bfloat16),
            pltpu.VMEM((own_rows, LANES), jnp.float32),
            pltpu.VMEM((4, chunks, 8, LANES), jnp.float32),
            pltpu.VMEM((4, groups // 8, 8, LANES), jnp.float32),
            pltpu.VMEM((chunks, 3, 8, LANES), jnp.int32),
            pltpu.SMEM(fetch_list.shape, jnp.int32),
            pltpu.SMEM(listed.shape, jnp.int32),
            pltpu.SMEM(counts.shape, jnp.int32),
            dma((owned,)),
            dma((3,)),
            dma((groups,)),
            dma((groups,)),
            dma((8,)),
            dma((8,)),
            dma((8,)),
            dma((8,)),
            dma((8,)),
            dma((8,)),
            dma((4,)),
            dma((4,)),
            dma((groups,)),
            dma((groups,)),
        ],
        compiler_params=pltpu.CompilerParams(
            collective_id=0, has_side_effects=True, vmem_limit_bytes=60 * 2**20
        ),
        cost_estimate=pl.CostEstimate(
            flops=flops, bytes_accessed=own_rows * width * 2, transcendentals=0
        ),
    )(embeds.reshape(own_rows // 16, 16, width), fetch_list, listed, counts)


def solution(mesh):
    in_specs = (P("gx", "gy", None), P(), P(), P())
    out_specs = P("gx", "gy")
    return jax.shard_map(
        on_device, mesh=mesh, in_specs=in_specs, out_specs=out_specs, check_vma=False
    )
```
